32 devices in a mesh: groups: 2 (over x), cuts: 8 (over z, y), expert: 2 (over core).
Axes of the slice: x: 2, y: 2, z: 4, core: 2. Of those that a mesh axis runs over, the one named last changes fastest.
Arguments:
- tokens: bfloat16 [4096, 3072], P(('groups', 'cuts', 'expert')), parts along dimension 0, may hold values from -6 to 6
- expert_ids: int32 [4096, 2], P(('groups', 'cuts', 'expert')), parts along dimension 0, may hold values from 0 to 7, as said below
- gate_scale: float32 [4096, 2], P(('groups', 'cuts', 'expert')), parts along dimension 0, may hold values from 0.1 to 0.9
- w_gate: bfloat16 [2, 3072, 16384], P('expert', None, 'cuts'), may hold values from -0.109375 to 0.109375
- w_up: bfloat16 [2, 3072, 16384], P('expert', None, 'cuts'), may hold values from -0.109375 to 0.109375
- w_down: bfloat16 [2, 16384, 3072], P('expert', 'cuts'), may hold values from -0.046875 to 0.046875
Outputs:
- moe_out: bfloat16 [4096, 3072], P(('groups', 'cuts', 'expert')), parts along dimension 0
The draws below stay inside these ranges and needn't reach their ends.
There are 2 independent parts, one for each index of `groups`. The reference program is written for one: setup_inputs(seed, part) draws one part's arguments, and reference() takes and returns one part's arrays. A program takes and returns all parts, laid end to end along the dimension named above; an argument that names none is the same for every part. Nothing has to cross between parts.
Inputs may be any that keep to these rules, and one draw needn't show every extreme that they name: `expert_ids`: each token names two different experts. In the 128 rows of one device at most 32 name any one expert below 2; in every draw one such expert is named by exactly 32 rows on every device.
All inputs are finite; a program needn't handle non-finite values.
Results may differ from the reference program's by a relative error of at most 0.0058.
Values may be sent and summed in bfloat16 or wider, within the bound.
A program may use at most 128 MiB of HBM per device.

```python
import jax
import jax.numpy as jnp
from jax import lax

D = 3072
FF = 16384
EXPERTS_ALL = 8
TOK_DEV = 128
CAP = 32
EXP_WIN = 2
TOKENS = 2048
N_EXPERT = 2


def draw_expert_ids(key, part):
    key = jax.random.fold_in(key, 11)
    blocks = TOKENS // TOK_DEV
    keys = jax.random.split(key, 7)
    hot_expert = jax.random.randint(keys[0], (), 0, EXP_WIN)
    shift_cold = jax.random.randint(keys[1], (), 1, EXP_WIN)
    cold_expert = (hot_expert + shift_cold) % EXP_WIN
    cold_count = jax.random.randint(keys[2], (blocks, 1), 1, CAP // 2 + 1)
    ranking = jax.vmap(lambda sub: jax.random.permutation(sub, TOK_DEV))(jax.random.split(keys[3], blocks))
    others = EXPERTS_ALL - EXP_WIN
    other_first = jax.random.randint(keys[4], (blocks, TOK_DEV), EXP_WIN, EXPERTS_ALL)
    stepping = jax.random.randint(keys[5], (blocks, TOK_DEV), 1, max(others, 2))
    other_second = EXP_WIN + (other_first - EXP_WIN + stepping) % others
    first = jnp.where(ranking < CAP, hot_expert, jnp.where(ranking < CAP + cold_count, cold_expert, other_first))
    second = jnp.where(ranking < CAP + cold_count, other_first, other_second)
    swapped = jax.random.randint(keys[6], (blocks, TOK_DEV), 0, 2)
    column_a = jnp.where(swapped == 1, second, first)
    column_b = jnp.where(swapped == 1, first, second)
    return jnp.stack([column_a, column_b], axis=-1).reshape(TOKENS, 2).astype(jnp.int32)


def level_of(own_key, dims, pieces, smallest, largest):
    level = 1.0
    for axis_at, blocks in pieces:
        draws = jax.random.uniform(jax.random.fold_in(jax.random.fold_in(own_key, 6), axis_at), (blocks,), jnp.float32, smallest / len(pieces), largest / len(pieces))
        level = level * jnp.repeat(jnp.exp(draws), dims[axis_at] // blocks).reshape((-1,) + (1,) * (len(dims) - 1 - axis_at))
    return level


def bell_draw(stream_key, shape, scale, reach, pieces=(), held_as=jnp.bfloat16):
    array = scale * jax.random.normal(stream_key, shape, jnp.float32)
    if pieces:
        array = array * level_of(stream_key, shape, pieces, -0.22, 0.18)
    return jnp.clip(array, -reach, reach).astype(held_as)


def setup_inputs(seed: int = 0, part: int = 0) -> dict:
    key_of = jax.random.split(jax.random.key(seed), 7)
    part_splits = jax.random.split(jax.random.fold_in(key_of[6], part), 7)
    tokens = bell_draw(part_splits[0], (TOKENS, D), 1.0, 6.0, ((0, 16),))
    expert_ids = draw_expert_ids(jax.random.fold_in(jax.random.fold_in(key_of[6], part), 71), part)
    gate_scale = jnp.clip(0.1 + 0.79999997 * jax.random.uniform(part_splits[2], (TOKENS, 2), jnp.float32) ** level_of(part_splits[2], (TOKENS, 2), ((0, 16),), -0.2, 0.2), 0.1, 0.9)
    w_gate = bell_draw(key_of[3], (EXP_WIN, D, FF), D ** -0.5, 0.109375, ((0, 2), (2, 8)))
    w_up = bell_draw(key_of[4], (EXP_WIN, D, FF), D ** -0.5, 0.109375, ((0, 2), (2, 8)))
    w_down = bell_draw(key_of[5], (EXP_WIN, FF, D), FF ** -0.5, 0.046875, ((0, 2), (1, 8)))
    return {"tokens": tokens, "expert_ids": expert_ids, "gate_scale": gate_scale, "w_gate": w_gate, "w_up": w_up, "w_down": w_down}


def routing(expert_ids, gate_scale, width, capacity):
    experts = jnp.arange(width, dtype=jnp.int32)
    named = expert_ids[:, :, None] == experts[None, None, :]
    member = jnp.any(named, axis=1).astype(jnp.int32)
    weight = jnp.sum(jnp.where(named, gate_scale[:, :, None], jnp.float32(0.0)), axis=1)
    before = jnp.cumsum(member, axis=0) - member
    slots = jnp.arange(capacity, dtype=jnp.int32)
    select = (member[:, :, None] == 1) & (before[:, :, None] == slots[None, None, :])
    return select.reshape(member.shape[0], width * capacity), weight


def reference(tokens, expert_ids, gate_scale, w_gate, w_up, w_down):
    width = N_EXPERT
    blocks = TOKENS // TOK_DEV
    tok_blocks = tokens.reshape(blocks, TOK_DEV, D)
    ids_blocks = expert_ids.reshape(blocks, TOK_DEV, 2)
    gate_blocks = gate_scale.reshape(blocks, TOK_DEV, 2)

    def make_buffer(rows, ids_here, gates_here):
        select, weight = routing(ids_here, gates_here, width, CAP)
        buffer = jnp.dot(select.astype(jnp.bfloat16).T, rows, preferred_element_type=jnp.float32)
        coef = select.astype(jnp.float32).reshape(TOK_DEV, width, CAP) * weight[:, :, None]
        return buffer.astype(jnp.bfloat16).reshape(width, CAP, D), coef.reshape(TOK_DEV, width * CAP)

    buffers, coefs = jax.vmap(make_buffer)(tok_blocks, ids_blocks, gate_blocks)
    outputs = []
    for expert in range(width):
        rows = buffers[:, expert].reshape(blocks * CAP, D)
        gate = jnp.dot(rows, w_gate[expert], preferred_element_type=jnp.float32)
        lin = jnp.dot(rows, w_up[expert], preferred_element_type=jnp.float32)
        hidden = (jax.nn.gelu(gate, approximate=False) * lin).astype(jnp.bfloat16)
        result = jnp.dot(hidden, w_down[expert], preferred_element_type=jnp.float32).astype(jnp.bfloat16)
        outputs.append(result.reshape(blocks, CAP, D))
    expert_rows = jnp.stack(outputs, axis=1).reshape(blocks, width * CAP, D)
    combined = jnp.einsum("bts,bsd->btd", coefs, expert_rows.astype(jnp.float32), precision=lax.Precision.HIGHEST)
    return combined.astype(jnp.bfloat16).reshape(TOKENS, D)
```

```python
import functools

import jax
import jax.numpy as jnp
from jax import lax
from jax.experimental import pallas as pl
from jax.experimental.pallas import tpu as pltpu
from jax.sharding import PartitionSpec as P

CAP = 32
SUB = 2
TILE = 256
MESH = pl.DeviceIdType.MESH


def ring_place(cut, n):
    side = cut % 2
    row = cut // 2
    return row + side * (n - 1 - 2 * row)


def ring_cut(place, n):
    back = place // (n // 2)
    return (1 - back) * (2 * place) + back * (2 * (n - 1 - place) + 1)


def kernel(n, tok, ids, gates, w_gate, w_up, w_down, out, wg, wu, wd, x, part, acc, fin, stage, hidden,
           w_sem, swap_send, swap_recv, ag_send, ag_recv, rs_send, rs_recv):
    half = n // 2
    core = lax.axis_index("expert")
    other = 1 - core
    place = ring_place(lax.axis_index("cuts"), n)
    right = ring_cut((place + 1) % n, n)
    left = ring_cut((place + n - 1) % n, n)
    toward = (right, left)

    barrier = pltpu.get_barrier_semaphore()
    for who in ({"expert": other}, {"cuts": right}, {"cuts": left},
                {"cuts": right, "expert": other}, {"cuts": left, "expert": other}):
        pl.semaphore_signal(barrier, inc=1, device_id=who, device_id_type=MESH)

    loads = []
    for at, (src, dst) in enumerate(((w_gate, wg), (w_up, wu), (w_down, wd))):
        rows = dst.shape[0] // 2
        pair = []
        for k in range(2):
            copy = pltpu.make_async_copy(src.at[0, pl.ds(k * rows, rows)], dst.at[pl.ds(k * rows, rows)], w_sem.at[at, k])
            copy.start()
            pair.append(copy)
        loads.append(pair)

    count = tok.shape[0]
    id_a, id_b = ids[:, 0:1], ids[:, 1:2]
    ga, gb = gates[:, 0:1], gates[:, 1:2]
    rows_at = lax.broadcasted_iota(jnp.int32, (count, count), 0)
    cols_at = lax.broadcasted_iota(jnp.int32, (count, count), 1)
    lower = jnp.where(cols_at < rows_at, 1.0, 0.0).astype(jnp.bfloat16)
    lanes = lax.broadcasted_iota(jnp.int32, (count, 128), 1)
    select = jnp.zeros((count, 128), jnp.float32)
    weights = []
    for at, e in enumerate((core, other)):
        hit_a, hit_b = id_a == e, id_b == e
        member = jnp.where(hit_a, 1.0, 0.0) + jnp.where(hit_b, 1.0, 0.0)
        weights.append(jnp.where(hit_a, ga, 0.0) + jnp.where(hit_b, gb, 0.0))
        member = jnp.broadcast_to(member, (count, 128))
        before = jnp.dot(lower, member.astype(jnp.bfloat16), preferred_element_type=jnp.float32)
        hit = (before + (at * CAP)) == lanes.astype(jnp.float32)
        inside = jnp.where(lanes >= at * CAP, 1.0, 0.0) * jnp.where(lanes < (at + 1) * CAP, 1.0, 0.0)
        select = select + jnp.where(hit, member, 0.0) * inside
    gather = select.T.astype(jnp.bfloat16)[: 2 * CAP]
    buf = jnp.dot(gather, tok[...], preferred_element_type=jnp.float32).astype(jnp.bfloat16)
    x[0, 0, 0] = buf[:CAP]
    stage[0] = buf[CAP:]

    pl.semaphore_wait(barrier, 5)

    started = []

    def remote(src, dst, ssem, rsem, who):
        return pltpu.make_async_remote_copy(src_ref=src, dst_ref=dst, send_sem=ssem, recv_sem=rsem,
                                            device_id=who, device_id_type=MESH)

    def xref(t, d, s):
        return x.at[t // 2, t % 2, d, pl.ds(s * (CAP // SUB), CAP // SUB)]

    def ag_copy(t, d, s):
        if t == 1:
            src = xref(0, d, s)
        elif t == half + 1:
            src = xref(0, 1 - d, s)
        else:
            src = xref(t - 1, d, s)
        return remote(src, xref(t, d, s), ag_send.at[d, t, s], ag_recv.at[d, t, s], {"cuts": toward[d]})

    def ag_start(t, d, s):
        copy = ag_copy(t, d, s)
        copy.start()
        started.append(copy)

    swap = remote(stage.at[0], x.at[0, 0, 1], swap_send.at[0], swap_recv.at[0], {"expert": other})
    swap.start()
    started.append(swap)
    for s in range(SUB):
        ag_start(1, 0, s)
    swap.wait_recv()
    for s in range(SUB):
        ag_start(1, 1, s)

    def ag(t):
        for s in range(SUB):
            for d in range(2):
                ag_copy(t, d, s).wait_recv()
                if t != half and t < n - 1:
                    ag_start(t + 1, d, s)
        if t == half - 1:
            for s in range(SUB):
                for d in range(2):
                    ag_start(half + 1, d, s)

    def up_part(j):
        if j == 0:
            for pair in loads[:2]:
                for copy in pair:
                    copy.wait()

        def body(c, carry):
            cols = pl.ds(pl.multiple_of(c * TILE, TILE), TILE)
            rows = x[j].reshape(4 * CAP, x.shape[-1])
            g = jnp.dot(rows, wg[:, cols], preferred_element_type=jnp.float32)
            u = jnp.dot(rows, wu[:, cols], preferred_element_type=jnp.float32)
            h = 0.5 * g * (1.0 + lax.erf(g * 0.7071067811865476)) * u
            hidden[:, cols] = h.astype(jnp.bfloat16)
            return carry

        lax.fori_loop(0, wg.shape[1] // TILE, body, 0)

    def down_part(j):
        if j == 0:
            for copy in loads[2]:
                copy.wait()

        def body(c, carry):
            cols = pl.ds(pl.multiple_of(c * TILE, TILE), TILE)
            r = jnp.dot(hidden[...], wd[:, cols], preferred_element_type=jnp.float32)
            part[j, :, :, :, cols] = r.astype(jnp.bfloat16).reshape(2, 2, CAP, TILE)
            return carry

        lax.fori_loop(0, wd.shape[1] // TILE, body, 0)

    def pref(t, d, s):
        return part.at[t // 2, t % 2, d, pl.ds(s * (CAP // SUB), CAP // SUB)]

    def own(chain, d, k, s):
        if chain == 0:
            return pref(k, 1 - d, s)
        if k == half:
            return pref(half, d, s)
        return pref(half + k, 1 - d, s)

    def top(chain):
        return half - 1 + chain

    def aref(chain, d, k, s):
        return acc.at[chain, d, k, pl.ds(s * (CAP // SUB), CAP // SUB)]

    def fref(h, d, s):
        return fin.at[h, d, pl.ds(s * (CAP // SUB), CAP // SUB)]

    def rs_copy(chain, d, k, s):
        src = own(chain, d, k, s) if k == top(chain) else aref(chain, d, k, s)
        h = (1 - chain) if d == 0 else chain
        ssem, rsem = rs_send.at[chain, d, k, s], rs_recv.at[chain, d, k, s]
        if k > 1:
            return remote(src, aref(chain, d, k - 1, s), ssem, rsem, {"cuts": toward[d]})
        if h == 0:
            return remote(src, fref(0, d, s), ssem, rsem, {"cuts": toward[d]})
        return remote(src, fref(1, d, s), ssem, rsem, {"cuts": toward[d], "expert": other})

    def rs_start(chain, d, k, s):
        copy = rs_copy(chain, d, k, s)
        copy.start()
        started.append(copy)

    def rs_open(chain):
        for s in range(SUB):
            for d in range(2):
                rs_start(chain, d, top(chain), s)

    def rs(chain, k):
        for s in range(SUB):
            for d in range(2):
                rs_copy(chain, d, k + 1, s).wait_recv()
                if k > 0:
                    a, b = aref(chain, d, k, s), own(chain, d, k, s)
                    a[...] = (a[...].astype(jnp.float32) + b[...].astype(jnp.float32)).astype(jnp.bfloat16)
                    rs_start(chain, d, k, s)

    own_swap = remote(part.at[0, 0, 1], stage.at[1], swap_send.at[1], swap_recv.at[1], {"expert": other})

    opened = 0
    for t in range(1, n):
        ag(t)
        if t >= 2 and t % 2 == 0:
            up_part(t // 2 - 1)
        if t >= 3 and t % 2 == 1:
            j = (t - 3) // 2
            down_part(j)
            if j == 0:
                own_swap.start()
                started.append(own_swap)
            if opened == 0 and 2 * j + 1 >= half - 1:
                rs_open(0)
                opened = 1
            if opened == 1 and 2 * j + 1 >= half:
                rs_open(1)
                opened = 2
    work = [functools.partial(up_part, half - 1), functools.partial(down_part, half - 1)]
    for k in range(half - 2, -1, -1):
        rs(0, k)
        if work:
            work.pop(0)()
    for item in work:
        item()
    for k in range(half - 1, -1, -1):
        rs(1, k)
    own_swap.wait_recv()

    keep = select.astype(jnp.bfloat16)
    first = fin[0, 0].astype(jnp.float32) + fin[0, 1].astype(jnp.float32) + part[0, 0, 0].astype(jnp.float32)
    second = fin[1, 0].astype(jnp.float32) + fin[1, 1].astype(jnp.float32) + stage[1].astype(jnp.float32)
    res = weights[0] * jnp.dot(keep[:, :CAP], first.astype(jnp.bfloat16), preferred_element_type=jnp.float32)
    res += weights[1] * jnp.dot(keep[:, CAP:2 * CAP], second.astype(jnp.bfloat16), preferred_element_type=jnp.float32)
    out[...] = res.astype(out.dtype)

    for copy in started:
        copy.wait_send()


def on_device(tokens, expert_ids, gate_scale, w_gate, w_up, w_down):
    n = lax.axis_size("cuts")
    half = n // 2
    feat = tokens.shape[1]
    ff = w_gate.shape[2]
    bf = jnp.bfloat16
    vmem = pl.BlockSpec(memory_space=pltpu.VMEM)
    hbm = pl.BlockSpec(memory_space=pl.ANY)
    dma = pltpu.SemaphoreType.DMA
    return pl.pallas_call(
        functools.partial(kernel, n),
        out_shape=jax.ShapeDtypeStruct(tokens.shape, bf),
        in_specs=[vmem, vmem, vmem, hbm, hbm, hbm],
        out_specs=vmem,
        scratch_shapes=[
            pltpu.VMEM((feat, ff), bf),
            pltpu.VMEM((feat, ff), bf),
            pltpu.VMEM((ff, feat), bf),
            pltpu.VMEM((half, 2, 2, CAP, feat), bf),
            pltpu.VMEM((half, 2, 2, CAP, feat), bf),
            pltpu.VMEM((2, 2, half, CAP, feat), bf),
            pltpu.VMEM((2, 2, CAP, feat), bf),
            pltpu.VMEM((2, CAP, feat), bf),
            pltpu.VMEM((4 * CAP, ff), bf),
            dma((3, 2)),
            dma((2,)),
            dma((2,)),
            dma((2, n, SUB)),
            dma((2, n, SUB)),
            dma((2, 2, half + 1, SUB)),
            dma((2, 2, half + 1, SUB)),
        ],
        compiler_params=pltpu.CompilerParams(
            collective_id=0, has_side_effects=True, vmem_limit_bytes=60 * 1024 * 1024
        ),
        name="moe_ring",
    )(tokens, expert_ids, gate_scale, w_gate, w_up, w_down)


def solution(mesh):
    placed = (
        P(("groups", "cuts", "expert"), None),
        P(("groups", "cuts", "expert"), None),
        P(("groups", "cuts", "expert"), None),
        P("expert", None, "cuts"),
        P("expert", None, "cuts"),
        P("expert", "cuts", None),
    )
    return jax.shard_map(
        on_device,
        mesh=mesh,
        in_specs=placed,
        out_specs=P(("groups", "cuts", "expert"), None),
        check_vma=False,
    )
```

```python
import functools

import jax
import jax.numpy as jnp
from jax import lax
from jax.experimental import pallas as pl
from jax.experimental.pallas import tpu as pltpu
from jax.sharding import PartitionSpec as P

CAP = 32
SUB = 2
TILE = 512
UP_BITS = 2
DOWN_BITS = 2
WARM = 3
MESH = pl.DeviceIdType.MESH


def ring_place(cut, n):
    side = cut % 2
    row = cut // 2
    return row + side * (n - 1 - 2 * row)


def ring_cut(place, n):
    back = place // (n // 2)
    return (1 - back) * (2 * place) + back * (2 * (n - 1 - place) + 1)


def kernel(n, tok_hbm, ids_hbm, gates_hbm, w_gate, w_up, w_down, out_hbm, tok, ids, gates, out, wg, wu, wd, x, part, acc, fin,
           stage, hidden, in_sem, out_sem, w_sem, swap_send, swap_recv, ag_send, ag_recv, rs_send, rs_recv):
    half = n // 2
    core = lax.axis_index("expert")
    other = 1 - core
    place = ring_place(lax.axis_index("cuts"), n)
    right = ring_cut((place + 1) % n, n)
    left = ring_cut((place + n - 1) % n, n)
    toward = (right, left)

    barrier = pltpu.get_barrier_semaphore()
    for who in ({"expert": other}, {"cuts": right}, {"cuts": left},
                {"cuts": right, "expert": other}, {"cuts": left, "expert": other}):
        pl.semaphore_signal(barrier, inc=1, device_id=who, device_id_type=MESH)

    brought = [pltpu.make_async_copy(src, dst, in_sem.at[at])
               for at, (src, dst) in enumerate(((ids_hbm, ids), (gates_hbm, gates), (tok_hbm, tok)))]
    for copy in brought:
        copy.start()

    count = tok.shape[0]
    feat = tok.shape[1]
    width = feat // SUB
    rows_at = lax.broadcasted_iota(jnp.int32, (count, count), 0)
    cols_at = lax.broadcasted_iota(jnp.int32, (count, count), 1)
    upper = jnp.where(rows_at < cols_at, 1.0, 0.0).astype(jnp.bfloat16)
    brought[0].wait()

    id_a, id_b = ids[0:1, :], ids[1:2, :]
    slots = lax.broadcasted_iota(jnp.int32, (CAP, count), 0).astype(jnp.float32)
    pieces = []
    for e in (core, other):
        member = jnp.where(id_a == e, 1.0, 0.0) + jnp.where(id_b == e, 1.0, 0.0)
        member = jnp.broadcast_to(member, (CAP, count))
        before = jnp.dot(member.astype(jnp.bfloat16), upper, preferred_element_type=jnp.float32)
        pieces.append(jnp.where(before == slots, member, 0.0))
    gather = jnp.concatenate(pieces, axis=0)
    brought[2].wait()
    loads = []
    for at, (src, dst) in enumerate(((w_gate, wg), (w_up, wu), (w_down, wd))):
        rows = dst.shape[0] // 2
        pair = []
        for k in range(2):
            copy = pltpu.make_async_copy(src.at[0, pl.ds(k * rows, rows)], dst.at[pl.ds(k * rows, rows)], w_sem.at[at, k])
            copy.start()
            pair.append(copy)
        loads.append(pair)
    buf = jnp.dot(gather.astype(jnp.bfloat16), tok[...], preferred_element_type=jnp.float32).astype(jnp.bfloat16)
    x[0, 0, 0] = buf[:CAP]
    stage[0] = buf[CAP:]

    pl.semaphore_wait(barrier, 5)

    started = []

    def remote(src, dst, ssem, rsem, who):
        return pltpu.make_async_remote_copy(src_ref=src, dst_ref=dst, send_sem=ssem, recv_sem=rsem,
                                            device_id=who, device_id_type=MESH)

    def xref(t, d, s):
        return x.at[t // 2, t % 2, d, :, pl.ds(s * width, width)]

    def ag_copy(t, d, s):
        if t == 1:
            src = xref(0, d, s)
        elif t == half + 1:
            src = xref(0, 1 - d, s)
        else:
            src = xref(t - 1, d, s)
        return remote(src, xref(t, d, s), ag_send.at[d, t, s], ag_recv.at[d, t, s], {"cuts": toward[d]})

    def ag_start(t, d, s):
        copy = ag_copy(t, d, s)
        copy.start()
        started.append(copy)

    swap = remote(stage.at[0], x.at[0, 0, 1], swap_send.at[0], swap_recv.at[0], {"expert": other})
    swap.start()
    started.append(swap)
    for s in range(SUB):
        ag_start(1, 0, s)
    swap.wait_recv()
    for s in range(SUB):
        ag_start(1, 1, s)

    def ag(t, s):
        for d in range(2):
            ag_copy(t, d, s).wait_recv()
            if t != half and t < n - 1:
                ag_start(t + 1, d, s)
        if t == half - 1:
            for d in range(2):
                ag_start(half + 1, d, s)

    def up_part(j, lo, hi):
        if j == 0 and lo == 0:
            for pair in loads[:2]:
                for copy in pair:
                    copy.wait()

        def body(c, carry):
            cols = pl.ds(pl.multiple_of(c * TILE, TILE), TILE)
            rows = x[j].reshape(4 * CAP, feat)
            g = jnp.dot(rows, wg[:, cols], preferred_element_type=jnp.float32)
            u = jnp.dot(rows, wu[:, cols], preferred_element_type=jnp.float32)
            h = 0.5 * g * (1.0 + lax.erf(g * 0.7071067811865476)) * u
            hidden[:, cols] = h.astype(jnp.bfloat16)
            return carry

        lax.fori_loop(lo, hi, body, 0)

    def down_part(j, lo, hi):
        if j == 0 and lo == 0:
            for copy in loads[2]:
                copy.wait()

        def body(c, carry):
            cols = pl.ds(pl.multiple_of(c * TILE, TILE), TILE)
            r = jnp.dot(hidden[...], wd[:, cols], preferred_element_type=jnp.float32)
            part[j, :, :, :, cols] = r.astype(jnp.bfloat16).reshape(2, 2, CAP, TILE)
            return carry

        lax.fori_loop(lo, hi, body, 0)

    def pref(t, d, s):
        return part.at[t // 2, t % 2, d, :, pl.ds(s * width, width)]

    def own(chain, d, k, s):
        if chain == 0:
            return pref(k, 1 - d, s)
        if k == half:
            return pref(half, d, s)
        return pref(half + k, 1 - d, s)

    def top(chain):
        return half - 1 + chain

    def aref(chain, d, k, s):
        return acc.at[chain, d, k, :, pl.ds(s * width, width)]

    def fref(h, d, s):
        return fin.at[h, d, :, pl.ds(s * width, width)]

    def rs_copy(chain, d, k, s):
        src = own(chain, d, k, s) if k == top(chain) else aref(chain, d, k, s)
        h = (1 - chain) if d == 0 else chain
        ssem, rsem = rs_send.at[chain, d, k, s], rs_recv.at[chain, d, k, s]
        if k > 1:
            return remote(src, aref(chain, d, k - 1, s), ssem, rsem, {"cuts": toward[d]})
        if h == 0:
            return remote(src, fref(0, d, s), ssem, rsem, {"cuts": toward[d]})
        return remote(src, fref(1, d, s), ssem, rsem, {"cuts": toward[d], "expert": other})

    def rs_start(chain, d, k, s):
        copy = rs_copy(chain, d, k, s)
        copy.start()
        started.append(copy)

    def rs_open(chain):
        for s in range(SUB):
            for d in range(2):
                rs_start(chain, d, top(chain), s)

    def rs(chain, k, s):
        for d in range(2):
            rs_copy(chain, d, k + 1, s).wait_recv()
            if k > 0:
                a, b = aref(chain, d, k, s), own(chain, d, k, s)
                a[...] = (a[...].astype(jnp.float32) + b[...].astype(jnp.float32)).astype(jnp.bfloat16)
                rs_start(chain, d, k, s)

    own_swap = remote(part.at[0, 0, 1], stage.at[1], swap_send.at[1], swap_recv.at[1], {"expert": other})

    def swap_own():
        own_swap.start()
        started.append(own_swap)

    ups, downs = wg.shape[1] // TILE, feat // TILE
    bits = []
    for j in range(half):
        cuts = [ups * k // UP_BITS for k in range(UP_BITS + 1)]
        bits += [(2 * j + 1, functools.partial(up_part, j, lo, hi)) for lo, hi in zip(cuts, cuts[1:]) if lo < hi]
        cuts = [downs * k // DOWN_BITS for k in range(DOWN_BITS + 1)]
        bits += [(2 * j + 1, functools.partial(down_part, j, lo, hi)) for lo, hi in zip(cuts, cuts[1:]) if lo < hi]
        bits.append((2 * j + 1, ("pass", j)))
    done = -1
    opened = 0

    def advance(reached):
        nonlocal done, opened
        if not bits or bits[0][0] > reached:
            return False
        bits.pop(0)[1]()
        if bits and isinstance(bits[0][1], tuple):
            done = bits.pop(0)[1][1]
            if done == 0:
                swap_own()
            if opened == 0 and 2 * done + 1 >= half - 1:
                rs_open(0)
                opened = 1
            if opened == 1 and 2 * done + 1 >= half:
                rs_open(1)
                opened = 2
        return True

    for t in range(1, n):
        for s in range(SUB):
            ag(t, s)
            if t >= WARM:
                advance(t if s == SUB - 1 else t - 1)
    while opened == 0:
        advance(n - 1)
    for k in range(half - 2, -1, -1):
        for s in range(SUB):
            rs(0, k, s)
            advance(n - 1)
    while bits:
        advance(n - 1)
    for k in range(half - 1, 0, -1):
        for s in range(SUB):
            rs(1, k, s)

    gates_copy = brought[1]
    gates_copy.wait()
    keep = jnp.concatenate([gather, jnp.zeros((count - 2 * CAP, count), jnp.float32)], axis=0).T.astype(jnp.bfloat16)
    spread = []
    for e in (core, other):
        w = jnp.where(id_a == e, gates[0:1, :], 0.0) + jnp.where(id_b == e, gates[1:2, :], 0.0)
        spread.append(jnp.broadcast_to(w, (count, count)).T[:, 0:1])
    own_swap.wait_recv()
    outs = []
    for s in range(SUB):
        cols = slice(s * width, (s + 1) * width)
        rs(1, 0, s)
        first = fin[0, 0, :, cols].astype(jnp.float32) + fin[0, 1, :, cols].astype(jnp.float32) + part[0, 0, 0, :, cols].astype(jnp.float32)
        second = fin[1, 0, :, cols].astype(jnp.float32) + fin[1, 1, :, cols].astype(jnp.float32) + stage[1, :, cols].astype(jnp.float32)
        res = spread[0] * jnp.dot(keep[:, :CAP], first.astype(jnp.bfloat16), preferred_element_type=jnp.float32)
        res += spread[1] * jnp.dot(keep[:, CAP:2 * CAP], second.astype(jnp.bfloat16), preferred_element_type=jnp.float32)
        out[:, cols] = res.astype(out.dtype)
        copy = pltpu.make_async_copy(out.at[:, pl.ds(s * width, width)], out_hbm.at[:, pl.ds(s * width, width)], out_sem.at[s])
        copy.start()
        outs.append(copy)
    for copy in outs:
        copy.wait()
    for copy in started:
        copy.wait_send()


def on_device(tokens, expert_ids, gate_scale, w_gate, w_up, w_down):
    n = lax.axis_size("cuts")
    half = n // 2
    feat = tokens.shape[1]
    ff = w_gate.shape[2]
    bf = jnp.bfloat16
    hbm = pl.BlockSpec(memory_space=pl.ANY)
    dma = pltpu.SemaphoreType.DMA
    return pl.pallas_call(
        functools.partial(kernel, n),
        out_shape=jax.ShapeDtypeStruct(tokens.shape, bf),
        in_specs=[hbm] * 6,
        out_specs=hbm,
        scratch_shapes=[
            pltpu.VMEM(tokens.shape, bf),
            pltpu.VMEM((2, tokens.shape[0]), jnp.int32),
            pltpu.VMEM((2, tokens.shape[0]), jnp.float32),
            pltpu.VMEM(tokens.shape, bf),
            pltpu.VMEM((feat, ff), bf),
            pltpu.VMEM((feat, ff), bf),
            pltpu.VMEM((ff, feat), bf),
            pltpu.VMEM((half, 2, 2, CAP, feat), bf),
            pltpu.VMEM((half, 2, 2, CAP, feat), bf),
            pltpu.VMEM((2, 2, half, CAP, feat), bf),
            pltpu.VMEM((2, 2, CAP, feat), bf),
            pltpu.VMEM((2, CAP, feat), bf),
            pltpu.VMEM((4 * CAP, ff), bf),
            dma((3,)),
            dma((SUB,)),
            dma((3, 2)),
            dma((2,)),
            dma((2,)),
            dma((2, n, SUB)),
            dma((2, n, SUB)),
            dma((2, 2, half + 1, SUB)),
            dma((2, 2, half + 1, SUB)),
        ],
        compiler_params=pltpu.CompilerParams(
            collective_id=0, has_side_effects=True, vmem_limit_bytes=60 * 1024 * 1024
        ),
        name="moe_ring",
    )(tokens, expert_ids.T, gate_scale.T, w_gate, w_up, w_down)


def solution(mesh):
    placed = (
        P(("groups", "cuts", "expert"), None),
        P(("groups", "cuts", "expert"), None),
        P(("groups", "cuts", "expert"), None),
        P("expert", None, "cuts"),
        P("expert", None, "cuts"),
        P("expert", "cuts", None),
    )
    return jax.shard_map(
        on_device,
        mesh=mesh,
        in_specs=placed,
        out_specs=P(("groups", "cuts", "expert"), None),
        check_vma=False,
    )
```

```python
import functools

import jax
import jax.numpy as jnp
from jax import lax
from jax.experimental import pallas as pl
from jax.experimental.pallas import tpu as pltpu
from jax.sharding import PartitionSpec as P

CAP = 32
SUB = 2
TILE = 512
UP_BITS = 2
DOWN_BITS = 2
WARM = 3
MESH = pl.DeviceIdType.MESH


def ring_place(cut, n):
    side = cut % 2
    row = cut // 2
    return row + side * (n - 1 - 2 * row)


def ring_cut(place, n):
    back = place // (n // 2)
    return (1 - back) * (2 * place) + back * (2 * (n - 1 - place) + 1)


def kernel(n, tok_hbm, ids_hbm, gates_hbm, w_gate, w_up, w_down, out_hbm, tok, ids, gates, out, wg, wu, wd, x, part, acc, fin,
           stage, hidden, in_sem, out_sem, w_sem, swap_send, swap_recv, ag_send, ag_recv, rs_send, rs_recv):
    half = n // 2
    core = lax.axis_index("expert")
    other = 1 - core
    place = ring_place(lax.axis_index("cuts"), n)
    right = ring_cut((place + 1) % n, n)
    left = ring_cut((place + n - 1) % n, n)
    toward = (right, left)

    barrier = pltpu.get_barrier_semaphore()
    for who in ({"expert": other}, {"cuts": right}, {"cuts": left},
                {"cuts": right, "expert": other}, {"cuts": left, "expert": other}):
        pl.semaphore_signal(barrier, inc=1, device_id=who, device_id_type=MESH)

    brought = [pltpu.make_async_copy(src, dst, in_sem.at[at])
               for at, (src, dst) in enumerate(((ids_hbm, ids), (gates_hbm, gates), (tok_hbm, tok)))]
    for copy in brought:
        copy.start()

    count = tok.shape[0]
    feat = tok.shape[1]
    width = feat // SUB
    rows_at = lax.broadcasted_iota(jnp.int32, (count, count), 0)
    cols_at = lax.broadcasted_iota(jnp.int32, (count, count), 1)
    upper = jnp.where(rows_at < cols_at, 1.0, 0.0).astype(jnp.bfloat16)
    brought[0].wait()

    id_a, id_b = ids[0:1, :], ids[1:2, :]
    slots = lax.broadcasted_iota(jnp.int32, (CAP, count), 0).astype(jnp.float32)
    pieces = []
    for e in (core, other):
        member = jnp.where(id_a == e, 1.0, 0.0) + jnp.where(id_b == e, 1.0, 0.0)
        member = jnp.broadcast_to(member, (CAP, count))
        before = jnp.dot(member.astype(jnp.bfloat16), upper, preferred_element_type=jnp.float32)
        pieces.append(jnp.where(before == slots, member, 0.0))
    gather = jnp.concatenate(pieces, axis=0)
    brought[2].wait()
    loads = []

    def load_start():
        for at, (src, dst) in enumerate(((w_gate, wg), (w_up, wu), (w_down, wd))):
            rows = dst.shape[0] // 2
            pair = []
            for k in range(2):
                copy = pltpu.make_async_copy(src.at[0, pl.ds(k * rows, rows)], dst.at[pl.ds(k * rows, rows)], w_sem.at[at, k])
                copy.start()
                pair.append(copy)
            loads.append(pair)

    chosen = gather.astype(jnp.bfloat16)
    pl.semaphore_wait(barrier, 5)

    started = []

    def remote(src, dst, ssem, rsem, who):
        return pltpu.make_async_remote_copy(src_ref=src, dst_ref=dst, send_sem=ssem, recv_sem=rsem,
                                            device_id=who, device_id_type=MESH)

    def xref(t, d, s):
        return x.at[t // 2, t % 2, d, :, pl.ds(s * width, width)]

    def ag_copy(t, d, s):
        if t == 1 and d == 1:
            return remote(stage.at[0, :, pl.ds(s * width, width)], xref(1, 1, s), ag_send.at[d, t, s], ag_recv.at[d, t, s],
                          {"cuts": left, "expert": other})
        if t == 1:
            src = xref(0, d, s)
        elif t == half + 1:
            src = xref(0, 1 - d, s)
        else:
            src = xref(t - 1, d, s)
        return remote(src, xref(t, d, s), ag_send.at[d, t, s], ag_recv.at[d, t, s], {"cuts": toward[d]})

    def ag_start(t, d, s):
        copy = ag_copy(t, d, s)
        copy.start()
        started.append(copy)

    for s in range(SUB):
        cols = slice(s * width, (s + 1) * width)
        buf = jnp.dot(chosen, tok[:, cols], preferred_element_type=jnp.float32).astype(jnp.bfloat16)
        x[0, 0, 0, :, cols] = buf[:CAP]
        stage[0, :, cols] = buf[CAP:]
        ag_start(1, 0, s)
        ag_start(1, 1, s)
    swap = remote(stage.at[0], x.at[0, 0, 1], swap_send.at[0], swap_recv.at[0], {"expert": other})
    swap.start()
    started.append(swap)
    load_start()
    swap.wait_recv()

    def ag(t, s):
        for d in range(2):
            ag_copy(t, d, s).wait_recv()
            if t != half and t < n - 1:
                ag_start(t + 1, d, s)
        if t == half - 1:
            for d in range(2):
                ag_start(half + 1, d, s)

    def up_part(j, lo, hi):
        if j == 0 and lo == 0:
            for pair in loads[:2]:
                for copy in pair:
                    copy.wait()

        def body(c, carry):
            cols = pl.ds(pl.multiple_of(c * TILE, TILE), TILE)
            rows = x[j].reshape(4 * CAP, feat)
            g = jnp.dot(rows, wg[:, cols], preferred_element_type=jnp.float32)
            u = jnp.dot(rows, wu[:, cols], preferred_element_type=jnp.float32)
            h = 0.5 * g * (1.0 + lax.erf(g * 0.7071067811865476)) * u
            hidden[:, cols] = h.astype(jnp.bfloat16)
            return carry

        lax.fori_loop(lo, hi, body, 0)

    def down_part(j, lo, hi):
        if j == 0 and lo == 0:
            for copy in loads[2]:
                copy.wait()

        def body(c, carry):
            cols = pl.ds(pl.multiple_of(c * TILE, TILE), TILE)
            r = jnp.dot(hidden[...], wd[:, cols], preferred_element_type=jnp.float32)
            part[j, :, :, :, cols] = r.astype(jnp.bfloat16).reshape(2, 2, CAP, TILE)
            return carry

        lax.fori_loop(lo, hi, body, 0)

    def pref(t, d, s):
        return part.at[t // 2, t % 2, d, :, pl.ds(s * width, width)]

    def own(chain, d, k, s):
        if chain == 0:
            return pref(k, 1 - d, s)
        if k == half:
            return pref(half, d, s)
        return pref(half + k, 1 - d, s)

    def top(chain):
        return half - 1 + chain

    def aref(chain, d, k, s):
        return acc.at[chain, d, k, :, pl.ds(s * width, width)]

    def fref(h, d, s):
        return fin.at[h, d, :, pl.ds(s * width, width)]

    def rs_copy(chain, d, k, s):
        src = own(chain, d, k, s) if k == top(chain) else aref(chain, d, k, s)
        h = (1 - chain) if d == 0 else chain
        ssem, rsem = rs_send.at[chain, d, k, s], rs_recv.at[chain, d, k, s]
        if k > 1:
            return remote(src, aref(chain, d, k - 1, s), ssem, rsem, {"cuts": toward[d]})
        if h == 0:
            return remote(src, fref(0, d, s), ssem, rsem, {"cuts": toward[d]})
        return remote(src, fref(1, d, s), ssem, rsem, {"cuts": toward[d], "expert": other})

    def rs_start(chain, d, k, s):
        copy = rs_copy(chain, d, k, s)
        copy.start()
        started.append(copy)

    def rs_open(chain):
        for s in range(SUB):
            for d in range(2):
                rs_start(chain, d, top(chain), s)

    def rs(chain, k, s):
        for d in range(2):
            rs_copy(chain, d, k + 1, s).wait_recv()
            if k > 0:
                a, b = aref(chain, d, k, s), own(chain, d, k, s)
                a[...] = (a[...].astype(jnp.float32) + b[...].astype(jnp.float32)).astype(jnp.bfloat16)
                rs_start(chain, d, k, s)

    own_swap = remote(part.at[0, 0, 1], stage.at[1], swap_send.at[1], swap_recv.at[1], {"expert": other})

    def swap_own():
        own_swap.start()
        started.append(own_swap)

    ups, downs = wg.shape[1] // TILE, feat // TILE
    bits = []
    for j in range(half):
        cuts = [ups * k // UP_BITS for k in range(UP_BITS + 1)]
        bits += [(2 * j + 1, functools.partial(up_part, j, lo, hi)) for lo, hi in zip(cuts, cuts[1:]) if lo < hi]
        cuts = [downs * k // DOWN_BITS for k in range(DOWN_BITS + 1)]
        bits += [(2 * j + 1, functools.partial(down_part, j, lo, hi)) for lo, hi in zip(cuts, cuts[1:]) if lo < hi]
        bits.append((2 * j + 1, ("pass", j)))
    done = -1
    opened = 0

    def advance(reached):
        nonlocal done, opened
        if not bits or bits[0][0] > reached:
            return False
        bits.pop(0)[1]()
        if bits and isinstance(bits[0][1], tuple):
            done = bits.pop(0)[1][1]
            if done == 0:
                swap_own()
            if opened == 0 and 2 * done + 1 >= half - 1:
                rs_open(0)
                opened = 1
            if opened == 1 and 2 * done + 1 >= half:
                rs_open(1)
                opened = 2
        return True

    for t in range(1, n):
        for s in range(SUB):
            ag(t, s)
            if t >= WARM:
                advance(t if s == SUB - 1 else t - 1)
    while opened == 0:
        advance(n - 1)
    for k in range(half - 2, 0, -1):
        for s in range(SUB):
            rs(0, k, s)
            advance(n - 1)
    while bits:
        advance(n - 1)
    for k in range(half - 1, 0, -1):
        for s in range(SUB):
            rs(1, k, s)

    gates_copy = brought[1]
    gates_copy.wait()
    keep = jnp.concatenate([gather, jnp.zeros((count - 2 * CAP, count), jnp.float32)], axis=0).T.astype(jnp.bfloat16)
    spread = []
    for e in (core, other):
        w = jnp.where(id_a == e, gates[0:1, :], 0.0) + jnp.where(id_b == e, gates[1:2, :], 0.0)
        spread.append(jnp.broadcast_to(w, (count, count)).T[:, 0:1])
    own_swap.wait_recv()
    outs = []
    for s in range(SUB):
        cols = slice(s * width, (s + 1) * width)
        rs(0, 0, s)
        rs(1, 0, s)
        first = fin[0, 0, :, cols].astype(jnp.float32) + fin[0, 1, :, cols].astype(jnp.float32) + part[0, 0, 0, :, cols].astype(jnp.float32)
        second = fin[1, 0, :, cols].astype(jnp.float32) + fin[1, 1, :, cols].astype(jnp.float32) + stage[1, :, cols].astype(jnp.float32)
        res = spread[0] * jnp.dot(keep[:, :CAP], first.astype(jnp.bfloat16), preferred_element_type=jnp.float32)
        res += spread[1] * jnp.dot(keep[:, CAP:2 * CAP], second.astype(jnp.bfloat16), preferred_element_type=jnp.float32)
        out[:, cols] = res.astype(out.dtype)
        copy = pltpu.make_async_copy(out.at[:, pl.ds(s * width, width)], out_hbm.at[:, pl.ds(s * width, width)], out_sem.at[s])
        copy.start()
        outs.append(copy)
    for copy in outs:
        copy.wait()
    for copy in started:
        copy.wait_send()


def on_device(tokens, expert_ids, gate_scale, w_gate, w_up, w_down):
    n = lax.axis_size("cuts")
    half = n // 2
    feat = tokens.shape[1]
    ff = w_gate.shape[2]
    bf = jnp.bfloat16
    hbm = pl.BlockSpec(memory_space=pl.ANY)
    dma = pltpu.SemaphoreType.DMA
    return pl.pallas_call(
        functools.partial(kernel, n),
        out_shape=jax.ShapeDtypeStruct(tokens.shape, bf),
        in_specs=[hbm] * 6,
        out_specs=hbm,
        scratch_shapes=[
            pltpu.VMEM(tokens.shape, bf),
            pltpu.VMEM((2, tokens.shape[0]), jnp.int32),
            pltpu.VMEM((2, tokens.shape[0]), jnp.float32),
            pltpu.VMEM(tokens.shape, bf),
            pltpu.VMEM((feat, ff), bf),
            pltpu.VMEM((feat, ff), bf),
            pltpu.VMEM((ff, feat), bf),
            pltpu.VMEM((half, 2, 2, CAP, feat), bf),
            pltpu.VMEM((half, 2, 2, CAP, feat), bf),
            pltpu.VMEM((2, 2, half, CAP, feat), bf),
            pltpu.VMEM((2, 2, CAP, feat), bf),
            pltpu.VMEM((2, CAP, feat), bf),
            pltpu.VMEM((4 * CAP, ff), bf),
            dma((3,)),
            dma((SUB,)),
            dma((3, 2)),
            dma((2,)),
            dma((2,)),
            dma((2, n, SUB)),
            dma((2, n, SUB)),
            dma((2, 2, half + 1, SUB)),
            dma((2, 2, half + 1, SUB)),
        ],
        compiler_params=pltpu.CompilerParams(
            collective_id=0, has_side_effects=True, vmem_limit_bytes=60 * 1024 * 1024
        ),
        name="moe_ring",
    )(tokens, expert_ids.T, gate_scale.T, w_gate, w_up, w_down)


def solution(mesh):
    placed = (
        P(("groups", "cuts", "expert"), None),
        P(("groups", "cuts", "expert"), None),
        P(("groups", "cuts", "expert"), None),
        P("expert", None, "cuts"),
        P("expert", None, "cuts"),
        P("expert", "cuts", None),
    )
    return jax.shard_map(
        on_device,
        mesh=mesh,
        in_specs=placed,
        out_specs=P(("groups", "cuts", "expert"), None),
        check_vma=False,
    )
```

```python
import functools

import jax
import jax.numpy as jnp
from jax import lax
from jax.experimental import pallas as pl
from jax.experimental.pallas import tpu as pltpu
from jax.sharding import PartitionSpec as P

CAP = 32
SUB = 2
TILE = 512
UP_BITS = 2
DOWN_BITS = 2
WARM = 2
MESH = pl.DeviceIdType.MESH


def ring_place(cut, n):
    side = cut % 2
    row = cut // 2
    return row + side * (n - 1 - 2 * row)


def ring_cut(place, n):
    back = place // (n // 2)
    return (1 - back) * (2 * place) + back * (2 * (n - 1 - place) + 1)


def kernel(n, tok_hbm, ids_hbm, gates_hbm, w_gate, w_up, w_down, out_hbm, tok, ids, gates, out, wg, wu, wd, x, part, acc, fin,
           stage, hidden, in_sem, out_sem, w_sem, swap_send, swap_recv, ag_send, ag_recv, rs_send, rs_recv):
    half = n // 2
    core = lax.axis_index("expert")
    other = 1 - core
    place = ring_place(lax.axis_index("cuts"), n)
    right = ring_cut((place + 1) % n, n)
    left = ring_cut((place + n - 1) % n, n)
    toward = (right, left)

    barrier = pltpu.get_barrier_semaphore()
    for who in ({"expert": other}, {"cuts": right}, {"cuts": left},
                {"cuts": right, "expert": other}, {"cuts": left, "expert": other}):
        pl.semaphore_signal(barrier, inc=1, device_id=who, device_id_type=MESH)

    brought = [pltpu.make_async_copy(src, dst, in_sem.at[at])
               for at, (src, dst) in enumerate(((ids_hbm, ids), (gates_hbm, gates), (tok_hbm, tok)))]
    for copy in brought:
        copy.start()

    count = tok.shape[0]
    feat = tok.shape[1]
    width = feat // SUB
    rows_at = lax.broadcasted_iota(jnp.int32, (count, count), 0)
    cols_at = lax.broadcasted_iota(jnp.int32, (count, count), 1)
    upper = jnp.where(rows_at < cols_at, 1.0, 0.0).astype(jnp.bfloat16)
    brought[0].wait()

    id_a, id_b = ids[0:1, :], ids[1:2, :]
    slots = lax.broadcasted_iota(jnp.int32, (CAP, count), 0).astype(jnp.float32)
    pieces = []
    for e in (core, other):
        member = jnp.where(id_a == e, 1.0, 0.0) + jnp.where(id_b == e, 1.0, 0.0)
        member = jnp.broadcast_to(member, (CAP, count))
        before = jnp.dot(member.astype(jnp.bfloat16), upper, preferred_element_type=jnp.float32)
        pieces.append(jnp.where(before == slots, member, 0.0))
    gather = jnp.concatenate(pieces, axis=0)
    brought[2].wait()
    loads = []

    def load_start():
        for at, (src, dst) in enumerate(((w_gate, wg), (w_up, wu), (w_down, wd))):
            cols = dst.shape[1] // 2
            loads.append([pltpu.make_async_copy(src.at[0, :, pl.ds(k * cols, cols)], dst.at[:, pl.ds(k * cols, cols)], w_sem.at[at, k])
                          for k in range(2)])
        for at, k in ((0, 0), (1, 0), (0, 1), (1, 1), (2, 0), (2, 1)):
            loads[at][k].start()

    chosen = gather.astype(jnp.bfloat16)
    pl.semaphore_wait(barrier, 5)

    started = []

    def remote(src, dst, ssem, rsem, who):
        return pltpu.make_async_remote_copy(src_ref=src, dst_ref=dst, send_sem=ssem, recv_sem=rsem,
                                            device_id=who, device_id_type=MESH)

    def xref(t, d, s):
        return x.at[t // 2, t % 2, d, :, pl.ds(s * width, width)]

    def ag_copy(t, d, s):
        if t == 1 and d == 1:
            return remote(stage.at[0, :, pl.ds(s * width, width)], xref(1, 1, s), ag_send.at[d, t, s], ag_recv.at[d, t, s],
                          {"cuts": left, "expert": other})
        if t == 1:
            src = xref(0, d, s)
        elif t == half + 1:
            src = xref(0, 1 - d, s)
        else:
            src = xref(t - 1, d, s)
        return remote(src, xref(t, d, s), ag_send.at[d, t, s], ag_recv.at[d, t, s], {"cuts": toward[d]})

    def ag_start(t, d, s):
        copy = ag_copy(t, d, s)
        copy.start()
        started.append(copy)

    for s in range(SUB):
        cols = slice(s * width, (s + 1) * width)
        buf = jnp.dot(chosen, tok[:, cols], preferred_element_type=jnp.float32).astype(jnp.bfloat16)
        x[0, 0, 0, :, cols] = buf[:CAP]
        stage[0, :, cols] = buf[CAP:]
        ag_start(1, 0, s)
        ag_start(1, 1, s)
    swap = remote(stage.at[0], x.at[0, 0, 1], swap_send.at[0], swap_recv.at[0], {"expert": other})
    swap.start()
    started.append(swap)
    load_start()
    swap.wait_recv()

    def ag(t, s):
        for d in range(2):
            ag_copy(t, d, s).wait_recv()
            if t != half and t < n - 1:
                ag_start(t + 1, d, s)
        if t == half - 1:
            for d in range(2):
                ag_start(half + 1, d, s)

    def up_part(j, lo, hi):
        if j == 0:
            for pair in loads[:2]:
                pair[0 if lo == 0 else 1].wait()

        def body(c, carry):
            cols = pl.ds(pl.multiple_of(c * TILE, TILE), TILE)
            rows = x[j].reshape(4 * CAP, feat)
            g = jnp.dot(rows, wg[:, cols], preferred_element_type=jnp.float32)
            u = jnp.dot(rows, wu[:, cols], preferred_element_type=jnp.float32)
            h = 0.5 * g * (1.0 + lax.erf(g * 0.7071067811865476)) * u
            hidden[:, cols] = h.astype(jnp.bfloat16)
            return carry

        lax.fori_loop(lo, hi, body, 0)

    def down_part(j, lo, hi):
        if j == 0:
            loads[2][0 if lo == 0 else 1].wait()

        def body(c, carry):
            cols = pl.ds(pl.multiple_of(c * TILE, TILE), TILE)
            r = jnp.dot(hidden[...], wd[:, cols], preferred_element_type=jnp.float32)
            part[j, :, :, :, cols] = r.astype(jnp.bfloat16).reshape(2, 2, CAP, TILE)
            return carry

        lax.fori_loop(lo, hi, body, 0)

    def pref(t, d, s):
        return part.at[t // 2, t % 2, d, :, pl.ds(s * width, width)]

    def own(chain, d, k, s):
        if chain == 0:
            return pref(k, 1 - d, s)
        if k == half:
            return pref(half, d, s)
        return pref(half + k, 1 - d, s)

    def top(chain):
        return half - 1 + chain

    def aref(chain, d, k, s):
        return acc.at[chain, d, k, :, pl.ds(s * width, width)]

    def fref(h, d, s):
        return fin.at[h, d, :, pl.ds(s * width, width)]

    def rs_copy(chain, d, k, s):
        src = own(chain, d, k, s) if k == top(chain) else aref(chain, d, k, s)
        h = (1 - chain) if d == 0 else chain
        ssem, rsem = rs_send.at[chain, d, k, s], rs_recv.at[chain, d, k, s]
        if k > 1:
            return remote(src, aref(chain, d, k - 1, s), ssem, rsem, {"cuts": toward[d]})
        if h == 0:
            return remote(src, fref(0, d, s), ssem, rsem, {"cuts": toward[d]})
        return remote(src, fref(1, d, s), ssem, rsem, {"cuts": toward[d], "expert": other})

    def rs_start(chain, d, k, s):
        copy = rs_copy(chain, d, k, s)
        copy.start()
        started.append(copy)

    def rs_open(chain):
        for s in range(SUB):
            for d in range(2):
                rs_start(chain, d, top(chain), s)

    def rs(chain, k, s):
        for d in range(2):
            rs_copy(chain, d, k + 1, s).wait_recv()
            if k > 0:
                a, b = aref(chain, d, k, s), own(chain, d, k, s)
                a[...] = (a[...].astype(jnp.float32) + b[...].astype(jnp.float32)).astype(jnp.bfloat16)
                rs_start(chain, d, k, s)

    own_swap = remote(part.at[0, 0, 1], stage.at[1], swap_send.at[1], swap_recv.at[1], {"expert": other})

    def swap_own():
        own_swap.start()
        started.append(own_swap)

    ups, downs = wg.shape[1] // TILE, feat // TILE
    bits = []
    for j in range(half):
        cuts = [ups * k // UP_BITS for k in range(UP_BITS + 1)]
        bits += [(2 * j + 1, functools.partial(up_part, j, lo, hi)) for lo, hi in zip(cuts, cuts[1:]) if lo < hi]
        cuts = [downs * k // DOWN_BITS for k in range(DOWN_BITS + 1)]
        bits += [(2 * j + 1, functools.partial(down_part, j, lo, hi)) for lo, hi in zip(cuts, cuts[1:]) if lo < hi]
        bits.append((2 * j + 1, ("pass", j)))
    done = -1
    opened = 0

    def advance(reached):
        nonlocal done, opened
        if not bits or bits[0][0] > reached:
            return False
        bits.pop(0)[1]()
        if bits and isinstance(bits[0][1], tuple):
            done = bits.pop(0)[1][1]
            if done == 0:
                swap_own()
            if opened == 0 and 2 * done + 1 >= half - 1:
                rs_open(0)
                opened = 1
            if opened == 1 and 2 * done + 1 >= half:
                rs_open(1)
                opened = 2
        return True

    for t in range(1, n):
        for s in range(SUB):
            ag(t, s)
            if t >= WARM:
                advance(t if s == SUB - 1 else t - 1)
    while opened == 0:
        advance(n - 1)
    for k in range(half - 2, 0, -1):
        for s in range(SUB):
            rs(0, k, s)
            advance(n - 1)
    while bits:
        advance(n - 1)
    for k in range(half - 1, 0, -1):
        for s in range(SUB):
            rs(1, k, s)

    gates_copy = brought[1]
    gates_copy.wait()
    keep = jnp.concatenate([gather, jnp.zeros((count - 2 * CAP, count), jnp.float32)], axis=0).T.astype(jnp.bfloat16)
    spread = []
    for e in (core, other):
        w = jnp.where(id_a == e, gates[0:1, :], 0.0) + jnp.where(id_b == e, gates[1:2, :], 0.0)
        spread.append(jnp.broadcast_to(w, (count, count)).T[:, 0:1])
    own_swap.wait_recv()
    outs = []
    for s in range(SUB):
        cols = slice(s * width, (s + 1) * width)
        rs(0, 0, s)
        rs(1, 0, s)
        first = fin[0, 0, :, cols].astype(jnp.float32) + fin[0, 1, :, cols].astype(jnp.float32) + part[0, 0, 0, :, cols].astype(jnp.float32)
        second = fin[1, 0, :, cols].astype(jnp.float32) + fin[1, 1, :, cols].astype(jnp.float32) + stage[1, :, cols].astype(jnp.float32)
        res = spread[0] * jnp.dot(keep[:, :CAP], first.astype(jnp.bfloat16), preferred_element_type=jnp.float32)
        res += spread[1] * jnp.dot(keep[:, CAP:2 * CAP], second.astype(jnp.bfloat16), preferred_element_type=jnp.float32)
        out[:, cols] = res.astype(out.dtype)
        copy = pltpu.make_async_copy(out.at[:, pl.ds(s * width, width)], out_hbm.at[:, pl.ds(s * width, width)], out_sem.at[s])
        copy.start()
        outs.append(copy)
    for copy in outs:
        copy.wait()
    for copy in started:
        copy.wait_send()


def on_device(tokens, expert_ids, gate_scale, w_gate, w_up, w_down):
    n = lax.axis_size("cuts")
    half = n // 2
    feat = tokens.shape[1]
    ff = w_gate.shape[2]
    bf = jnp.bfloat16
    hbm = pl.BlockSpec(memory_space=pl.ANY)
    dma = pltpu.SemaphoreType.DMA
    return pl.pallas_call(
        functools.partial(kernel, n),
        out_shape=jax.ShapeDtypeStruct(tokens.shape, bf),
        in_specs=[hbm] * 6,
        out_specs=hbm,
        scratch_shapes=[
            pltpu.VMEM(tokens.shape, bf),
            pltpu.VMEM((2, tokens.shape[0]), jnp.int32),
            pltpu.VMEM((2, tokens.shape[0]), jnp.float32),
            pltpu.VMEM(tokens.shape, bf),
            pltpu.VMEM((feat, ff), bf),
            pltpu.VMEM((feat, ff), bf),
            pltpu.VMEM((ff, feat), bf),
            pltpu.VMEM((half, 2, 2, CAP, feat), bf),
            pltpu.VMEM((half, 2, 2, CAP, feat), bf),
            pltpu.VMEM((2, 2, half, CAP, feat), bf),
            pltpu.VMEM((2, 2, CAP, feat), bf),
            pltpu.VMEM((2, CAP, feat), bf),
            pltpu.VMEM((4 * CAP, ff), bf),
            dma((3,)),
            dma((SUB,)),
            dma((3, 2)),
            dma((2,)),
            dma((2,)),
            dma((2, n, SUB)),
            dma((2, n, SUB)),
            dma((2, 2, half + 1, SUB)),
            dma((2, 2, half + 1, SUB)),
        ],
        compiler_params=pltpu.CompilerParams(
            collective_id=0, has_side_effects=True, vmem_limit_bytes=60 * 1024 * 1024
        ),
        name="moe_ring",
    )(tokens, expert_ids.T, gate_scale.T, w_gate, w_up, w_down)


def solution(mesh):
    placed = (
        P(("groups", "cuts", "expert"), None),
        P(("groups", "cuts", "expert"), None),
        P(("groups", "cuts", "expert"), None),
        P("expert", None, "cuts"),
        P("expert", None, "cuts"),
        P("expert", "cuts", None),
    )
    return jax.shard_map(
        on_device,
        mesh=mesh,
        in_specs=placed,
        out_specs=P(("groups", "cuts", "expert"), None),
        check_vma=False,
    )
```
